128 devices in a mesh: node: 2 (over z_lo), tm: 16 (over z_hi, x, core), space: 4 (over y).
Axes of the slice: x: 4, y: 4, z: 4 (z_hi: 2, z_lo: 2; z = z_hi * 2 + z_lo), core: 2. Of those that a mesh axis runs over, the one named last changes fastest.
Arguments:
- nodes: float32 [16, 4, 32, 256, 256], P('tm', 'node', 'space'), may hold values from -1.5 to 1.5
- prev_final: float32 [16, 32, 256, 256], P('tm', 'space'), may hold values from -6 to 6
- u_init: float32 [32, 256, 256], P('space'), may hold values from -6 to 6
- conductivity: float32 [32, 256, 256], P('space'), may hold values from 0.25 to 16
Outputs:
- new_nodes: float32 [16, 4, 32, 256, 256], P('tm', 'node', 'space')
The draws below stay inside these ranges and needn't reach their ends.
All inputs are finite; a program needn't handle non-finite values.
Results may differ from the reference program's by a relative error of at most 0.0003.
Values sent between devices are 32-bit elements; how exact they have to be, the bound alone decides.
No kernel may reach another device: no remote copies, remote signals or barrier semaphores. Data moves between devices by JAX's collectives and lax.ppermute only.
A program may use at most 128 MiB of HBM per device.

```python
import jax
import jax.numpy as jnp
from jax import lax

NY = 256
NZ = 256
NODES = 4
SWEEPS = 8
BLOCKS = 16
NX = 32


def draw_nodes(key, part):
    full_shape = (BLOCKS, NODES, NX, NY, NZ)
    x_index = lax.broadcasted_iota(jnp.int32, full_shape, 2)
    y_index = lax.broadcasted_iota(jnp.int32, full_shape, 3)
    z_index = lax.broadcasted_iota(jnp.int32, full_shape, 4)
    parity_sign = (1 - 2 * ((x_index + y_index + z_index) % 2)).astype(jnp.float32)
    magnitude = 1.0 + 0.25 * jnp.clip(jax.random.normal(key, full_shape, jnp.float32), -2.0, 2.0)
    return parity_sign * magnitude


def draw_conductivity(key, part):
    full_shape = (NX, NY, NZ)
    y_index = lax.broadcasted_iota(jnp.int32, full_shape, 1)
    z_index = lax.broadcasted_iota(jnp.int32, full_shape, 2)
    channel = (y_index + z_index) % 2 == 0
    key_high = jax.random.fold_in(key, 11)
    key_low = jax.random.fold_in(key, 23)
    high_values = 8.0 * jnp.exp(0.6931472 * jax.random.uniform(key_high, full_shape, jnp.float32, 0.0, 1.0))
    low_values = 0.25 * jnp.exp(0.6931472 * jax.random.uniform(key_low, full_shape, jnp.float32, 0.0, 1.0))
    return jnp.clip(jnp.where(channel, high_values, low_values), 0.25, 16.0)


def steps_of(key, shape, shards, least, high):
    def one(axis_at, parts):
        steps = jax.random.uniform(jax.random.fold_in(jax.random.fold_in(key, 6), axis_at), (parts,), jnp.float32, least / len(shards), high / len(shards))
        return jnp.repeat(jnp.exp(steps), shape[axis_at] // parts).reshape((-1,) + (1,) * (len(shape) - axis_at - 1))

    factor_of = one(*shards[0])
    for cut in shards[1:]:
        factor_of = factor_of * one(*cut)
    return factor_of


def centred(own_key, dims, scale, reach, pieces=(), dtype=jnp.bfloat16):
    values = scale * jax.random.normal(own_key, dims, jnp.float32)
    if pieces:
        values = values * steps_of(own_key, dims, pieces, -0.22, 0.18)
    return jnp.clip(values, -reach, reach).astype(dtype)


def setup_inputs(seed: int = 0) -> dict:
    arg_keys = jax.random.split(jax.random.key(seed), 5)
    nodes = draw_nodes(jax.random.fold_in(arg_keys[4], 71), 0)
    prev_final = centred(arg_keys[1], (BLOCKS, NX, NY, NZ), 1.0, 6.0, ((0, 16), (1, 4)), jnp.float32)
    u_init = centred(arg_keys[2], (NX, NY, NZ), 1.0, 6.0, ((0, 4),), jnp.float32)
    conductivity = draw_conductivity(jax.random.fold_in(arg_keys[4], 71), 0)
    return {"nodes": nodes, "prev_final": prev_final, "u_init": u_init, "conductivity": conductivity}


radau_points = [0.08858795951270394, 0.40946686444073470, 0.78765946176084705, 1.0]


def mixing_table():
    count_nodes = len(radau_points)
    table = [[0.0] * count_nodes for row_index in range(count_nodes)]
    for column in range(count_nodes):
        coefs = [1.0]
        for other in range(count_nodes):
            if other != column:
                scale = 1.0 / (radau_points[column] - radau_points[other])
                shifted = [0.0] + coefs
                lowered = [value * radau_points[other] for value in coefs] + [0.0]
                coefs = [(shifted[k] - lowered[k]) * scale for k in range(len(shifted))]
        for row_index in range(count_nodes):
            point = radau_points[row_index]
            integral = 0.0
            for power in range(len(coefs)):
                integral = integral + coefs[power] * point ** (power + 1) / (power + 1)
            table[row_index][column] = integral
        table[column][column] = table[column][column] - radau_points[column]
    return table


def from_lower(values, axis):
    axis = axis % values.ndim
    widths = [(0, 0)] * values.ndim
    widths[axis] = (1, 0)
    return lax.slice_in_dim(jnp.pad(values, widths), 0, values.shape[axis], axis=axis)


def from_upper(values, axis):
    axis = axis % values.ndim
    widths = [(0, 0)] * values.ndim
    widths[axis] = (0, 1)
    return lax.slice_in_dim(jnp.pad(values, widths), 1, values.shape[axis] + 1, axis=axis)


def coefficients(conduct_ext):
    centre = conduct_ext[1:-1]
    face_xl = 0.5 * (centre + conduct_ext[:-2])
    face_xr = 0.5 * (centre + conduct_ext[2:])
    padded_y = jnp.pad(centre, ((0, 0), (1, 1), (0, 0)), mode="edge")
    face_yl = 0.5 * (centre + padded_y[:, :-2])
    face_yr = 0.5 * (centre + padded_y[:, 2:])
    padded_z = jnp.pad(centre, ((0, 0), (0, 0), (1, 1)), mode="edge")
    face_zl = 0.5 * (centre + padded_z[:, :, :-2])
    face_zr = 0.5 * (centre + padded_z[:, :, 2:])
    summed = face_xl + face_xr + face_yl + face_yr + face_zl + face_zr
    return (face_xl, face_xr, face_yl, face_yr, face_zl, face_zr, summed)


def neighbours(padded, faces):
    centre = padded[..., 1:-1, :, :]
    result = faces[0] * padded[..., :-2, :, :] + faces[1] * padded[..., 2:, :, :]
    result = result + faces[2] * from_lower(centre, -2) + faces[3] * from_upper(centre, -2)
    result = result + faces[4] * from_lower(centre, -1) + faces[5] * from_upper(centre, -1)
    return result


def reference(nodes, prev_final, u_init, conductivity):
    faces = coefficients(jnp.pad(conductivity, ((1, 1), (0, 0), (0, 0)), mode="edge"))
    weights = jnp.asarray(mixing_table(), jnp.float32)
    node_diag = jnp.asarray(radau_points, jnp.float32)[:, None, None, None]
    starts = jnp.concatenate([u_init[None], prev_final[:-1]], axis=0)
    divisor = 1.0 + node_diag * faces[6]

    def block(pair):
        current, block_start = pair
        padded = jnp.pad(current, ((0, 0), (1, 1), (0, 0), (0, 0)))
        fluxes = neighbours(padded, faces) - faces[6] * current
        right_side = block_start[None] + jnp.einsum("mj,jxyz->mxyz", weights, fluxes, precision=lax.Precision.HIGHEST)
        iterate = current
        for repeat_index in range(SWEEPS):
            padded = jnp.pad(iterate, ((0, 0), (1, 1), (0, 0), (0, 0)))
            iterate = (right_side + node_diag * neighbours(padded, faces)) / divisor
        return iterate

    return lax.map(block, (nodes, starts))
```

```python
import functools

import jax
import jax.numpy as jnp
from jax import lax
from jax.experimental import pallas as pl
from jax.experimental.pallas import tpu as pltpu
from jax.sharding import PartitionSpec as P

radau_points = [0.08858795951270394, 0.4094668644407347, 0.787659461760847, 1.0]

Q = 17
ROWS = 8 * Q
PARTS = ((0, 0, 128), (120, 8, 128))
NY = 256
NZ = 256
PLANES = 8
F32 = jnp.float32


def mixing_table():
    count_nodes = len(radau_points)
    table = [[0.0] * count_nodes for row_index in range(count_nodes)]
    for column in range(count_nodes):
        coefs = [1.0]
        for other in range(count_nodes):
            if other != column:
                scale = 1.0 / (radau_points[column] - radau_points[other])
                shifted = [0.0] + coefs
                lowered = [value * radau_points[other] for value in coefs] + [0.0]
                coefs = [(shifted[k] - lowered[k]) * scale for k in range(len(shifted))]
        for row_index in range(count_nodes):
            point = radau_points[row_index]
            integral = 0.0
            for power in range(len(coefs)):
                integral = integral + coefs[power] * point ** (power + 1) / (power + 1)
            table[row_index][column] = integral
        table[column][column] = table[column][column] - radau_points[column]
    return table


WEIGHTS = mixing_table()

ANY = pl.BlockSpec(memory_space=pl.ANY)
VM = pl.BlockSpec(memory_space=pltpu.VMEM)


def vshape(planes):
    return pltpu.VMEM((planes, Q, 8, NZ), F32)


HB = pl.BlockSpec(memory_space=pltpu.HBM)


def pin(x):
    return pltpu.with_memory_space_constraint(x, pltpu.VMEM)


def place(x, where):
    if where is False:
        return x
    return pin(x) if where else pltpu.with_memory_space_constraint(x, pltpu.HBM)


TOKEN = pltpu.VMEM((8, 128), F32)


def with_token(kernel):
    def run(before, *refs):
        ins = refs[: run.ins]
        rest = refs[run.ins + run.skip :]
        rest[run.outs][...] = before[...]
        kernel(*ins, *rest[: run.outs], *rest[run.outs + 1 :])

    return run


class Order:
    def __init__(self):
        self.token = jnp.zeros((8, 128), F32)

    def call(self, name, kernel, outs, ins, scratch, limit_mib, us, aliases=None, after=()):
        run = with_token(kernel)
        run.ins, run.outs, run.skip = len(ins), len(outs), len(after)
        ins = ins + [(a, False) for a in after]
        operands = [pin(self.token)] + [place(a, where) for a, where in ins]
        *results, self.token = pl.pallas_call(
            run,
            out_shape=[o if s is VM else jax.ShapeDtypeStruct(o, F32) for o, s in outs] + [TOKEN],
            in_specs=[VM] + [{True: VM, None: HB, False: ANY}[where] for a, where in ins],
            out_specs=[s for o, s in outs] + [VM],
            scratch_shapes=scratch,
            input_output_aliases={k + 1: v for k, v in (aliases or {}).items()},
            compiler_params=pltpu.CompilerParams(vmem_limit_bytes=limit_mib << 20),
            cost_estimate=pl.CostEstimate(flops=int(us * 1e9), bytes_accessed=0, transcendentals=0),
            name=name,
        )(*operands)
        return results


SCALE = 1_500_000


def zprev(v):
    return pltpu.roll(v, 1, axis=1)


def znext(v):
    return pltpu.roll(v, NZ - 1, axis=1)


def sdown(v):
    return pltpu.roll(v, 1, axis=0)


def sup(v):
    return pltpu.roll(v, 7, axis=0)


def rows_of(buf, plane, r):
    return jnp.concatenate([buf[lane, plane, pl.ds(r, 8, stride=Q), :] for lane in range(2)], axis=-1)


def lane_copies(src_plane, dst_plane, sems):
    return [
        pltpu.make_async_copy(src_plane.at[:, pl.ds(128 * lane, 128)], dst_plane(lane), sems.at[lane])
        for lane in range(2)
    ]


def pick(table_low, table_high, node):
    return jnp.where(node == 0, jnp.float32(table_low), jnp.float32(table_high))


def own_scale(m, node):
    return pick(radau_points[m], radau_points[2 + m], node)


def inv_scale(m, node):
    return pick(1.0 / radau_points[m], 1.0 / radau_points[2 + m], node)


def weights_for(node):
    remote = [[pick(WEIGHTS[2 + m][j], WEIGHTS[m][2 + j], node) for j in range(2)] for m in range(2)]
    local = [[pick(WEIGHTS[m][j], WEIGHTS[2 + m][2 + j], node) for j in range(2)] for m in range(2)]
    return remote, local


class Rows:
    def __init__(self, k_at, y0):
        self.k_at = k_at
        self.first = y0 == 0
        self.last = y0 + ROWS == NY
        sub = lax.broadcasted_iota(jnp.int32, (8, NZ), 0)
        lane = lax.broadcasted_iota(jnp.int32, (8, NZ), 1)
        self.top = sub == 0
        self.bottom = sub == 7
        self.left = lane == 0
        self.right = lane == NZ - 1
        kc = k_at(0)
        kb = sdown(k_at(Q - 1))
        face = 0.5 * (kb + kc)
        if self.first:
            self.prev_sum = jnp.where(self.top, kc, face)
            self.prev = jnp.where(self.top, 0.0, face)
        else:
            self.prev_sum = face
            self.prev = face
        self.kc = kc

    def step(self, r):
        kc = self.kc
        kn = self.k_at(r + 1) if r < Q - 1 else sup(self.k_at(0))
        face = 0.5 * (kc + kn)
        face_sum = face
        if r == Q - 1:
            if self.last:
                face_sum = jnp.where(self.bottom, kc, face)
            face = jnp.where(self.bottom, 0.0, face)
        zface = 0.5 * (kc + znext(kc))
        zsum = jnp.where(self.right, kc, zface) + jnp.where(self.left, kc, zprev(zface))
        zface = jnp.where(self.right, 0.0, zface)
        total = self.prev_sum + face_sum + zsum
        below = self.prev
        self.prev = face
        self.prev_sum = face_sum
        self.kc = kn
        return kc, below, face, zface, total


def flux_rows(k_at, k_low, k_up, us, u_low, u_up, y0, emit):
    rows = Rows(k_at, y0)
    state = [(u(0), sdown(u(Q - 1))) for u in us]
    for r in range(Q):
        kc, below, face, zface, total = rows.step(r)
        fxl = 0.5 * (kc + k_low(r))
        fxu = 0.5 * (kc + k_up(r))
        total = total + (fxl + fxu)
        fluxes = []
        for j in range(2):
            uc, ub = state[j]
            un = us[j](r + 1) if r < Q - 1 else sup(us[j](0))
            n = fxl * u_low[j](r) + fxu * u_up[j](r)
            n = n + below * ub + face * un
            n = n + zface * znext(uc) + zprev(zface * uc)
            fluxes.append(n - total * uc)
            state[j] = (un, uc)
        emit(r, fluxes)


def inner_kernel(y0, offset0, offset1, nodes, cond, u0, kp, rem0, rem1, loc0, loc1, buf, sems):
    node = lax.axis_index("node")
    remote, local = weights_for(node)
    sources = [nodes.at[0, 0], nodes.at[0, 1], cond]

    def copies(p):
        out = []
        for a in range(3):
            out += lane_copies(
                sources[a].at[p, pl.ds(y0, ROWS), :], lambda lane, a=a: buf.at[lane, 3 * p + a], sems.at[p, a]
            )
        return out

    for p in range(PLANES):
        for c in copies(p):
            c.start()

    def convert(p, carry):
        for c in copies(p):
            c.wait()
        for r in range(Q):
            u0[p, r] = rows_of(buf, 3 * p, r)
            u0[PLANES + p, r] = rows_of(buf, 3 * p + 1, r)
            kp[p, r] = rows_of(buf, 3 * p + 2, r)
        return carry

    lax.fori_loop(0, PLANES, convert, 0)

    def plane(i, carry):
        p = i + 1

        def emit(r, f):
            rem0[i + offset0, r] = remote[0][0] * f[0] + remote[0][1] * f[1]
            rem1[i + offset1, r] = remote[1][0] * f[0] + remote[1][1] * f[1]
            loc0[i, r] = local[0][0] * f[0] + local[0][1] * f[1]
            loc1[i, r] = local[1][0] * f[0] + local[1][1] * f[1]

        at = lambda j, d: (lambda r: u0[j * PLANES + p + d, r])
        flux_rows(
            lambda r: kp[p, r],
            lambda r: kp[p - 1, r],
            lambda r: kp[p + 1, r],
            [at(0, 0), at(1, 0)],
            [at(0, -1), at(1, -1)],
            [at(0, 1), at(1, 1)],
            y0,
            emit,
        )
        return carry

    lax.fori_loop(0, PLANES - 2, plane, 0)


def faces_kernel(nodes, cond, na, nb, fa, fb, sems):
    even = lax.rem(lax.axis_index("space"), 2) == 0

    def copies(high_near, high_far, low_near, low_far):
        pairs = []
        for (near, far), (first, second) in (((high_near, high_far), (PLANES - 1, PLANES - 2)), ((low_near, low_far), (0, 1))):
            pairs += [(cond.at[first], near.at[0]), (cond.at[second], far.at[0])]
            for j in range(2):
                pairs += [(nodes.at[0, j, first], near.at[1 + j]), (nodes.at[0, j, second], far.at[1 + j])]
        return [pltpu.make_async_copy(src, dst, sems.at[i]) for i, (src, dst) in enumerate(pairs)]

    @pl.when(even)
    def _():
        for c in copies(na, fa, nb, fb):
            c.start()

    @pl.when(jnp.logical_not(even))
    def _():
        for c in copies(nb, fb, na, fa):
            c.start()

    for c in copies(na, fa, nb, fb):
        c.wait()


def halo_copies(near, planes, y0, buf, base, sems):
    out = []
    for i, p in enumerate(planes):
        out += lane_copies(
            near.at[p, pl.ds(y0, ROWS), :], lambda lane, i=i: buf.at[lane, base + i], sems.at[base + i]
        )
    return out


def begin_halos(na, nb, planes, y0, buf, sems):
    even = lax.rem(lax.axis_index("space"), 2) == 0
    n = len(planes)

    @pl.when(even)
    def _():
        for c in halo_copies(nb, planes, y0, buf, 0, sems) + halo_copies(na, planes, y0, buf, n, sems):
            c.start()

    @pl.when(jnp.logical_not(even))
    def _():
        for c in halo_copies(na, planes, y0, buf, 0, sems) + halo_copies(nb, planes, y0, buf, n, sems):
            c.start()


def end_halos(na, nb, planes, y0, buf, sems):
    for c in halo_copies(na, planes, y0, buf, 0, sems) + halo_copies(nb, planes, y0, buf, len(planes), sems):
        c.wait()


def edge_kernel(y0, at0, at1, u0, kp, na, nb, *refs):
    rem0, rem1, loc0, loc1, buf, hu, sems = refs[-7:]
    node = lax.axis_index("node")
    pos = lax.axis_index("space")
    remote, local = weights_for(node)
    planes = (0, 1, 2)
    begin_halos(na, nb, planes, y0, buf, sems)
    end_halos(na, nb, planes, y0, buf, sems)

    def convert(i, carry):
        for r in range(Q):
            hu[i, r] = rows_of(buf, i, r)
        return carry

    lax.fori_loop(0, 6, convert, 0)

    @pl.when(pos == 0)
    def _():
        hu[0] = kp[0]

    @pl.when(pos == 3)
    def _():
        hu[3] = kp[PLANES - 1]

    for e in range(2):
        p = 7 * e

        def emit(r, f, e=e):
            rem0[at0[e], r] = remote[0][0] * f[0] + remote[0][1] * f[1]
            rem1[at1[e], r] = remote[1][0] * f[0] + remote[1][1] * f[1]
            loc0[e, r] = local[0][0] * f[0] + local[0][1] * f[1]
            loc1[e, r] = local[1][0] * f[0] + local[1][1] * f[1]

        at = lambda j, d, p=p: (lambda r: u0[j * PLANES + p + d, r])
        kat = lambda d, p=p: (lambda r: kp[p + d, r])
        halo = lambda i, e=e: (lambda r: hu[3 * e + i, r])
        flux_rows(
            kat(0),
            kat(-1) if e else halo(0),
            halo(0) if e else kat(1),
            [at(0, 0), at(1, 0)],
            [at(0, -1), at(1, -1)] if e else [halo(1), halo(2)],
            [halo(1), halo(2)] if e else [at(0, 1), at(1, 1)],
            y0,
            emit,
        )


def coef_kernel(y0, kp, na, nb, fa, fb, fx, fy, fz, a0, a1, buf, far, kx, sems, far_sems):
    node = lax.axis_index("node")
    pos = lax.axis_index("space")
    begin_halos(na, nb, (0,), y0, buf, sems)
    begin_halos(fa, fb, (0,), y0, far, far_sems)

    def keep(p, carry):
        kx[p + 2] = kp[p]
        return carry

    lax.fori_loop(0, PLANES, keep, 0)
    end_halos(na, nb, (0,), y0, buf, sems)
    end_halos(fa, fb, (0,), y0, far, far_sems)

    @pl.when(pos > 0)
    def _():
        for r in range(Q):
            kx[0, r] = rows_of(far, 0, r)
            kx[1, r] = rows_of(buf, 0, r)

    @pl.when(pos == 0)
    def _():
        kx[0] = kp[0]
        kx[1] = kp[0]

    @pl.when(pos < 3)
    def _():
        for r in range(Q):
            kx[10, r] = rows_of(buf, 1, r)
            kx[11, r] = rows_of(far, 1, r)

    @pl.when(pos == 3)
    def _():
        kx[10] = kp[7]
        kx[11] = kp[7]

    inv0, inv1 = inv_scale(0, node), inv_scale(1, node)

    def coef(i, carry):
        rim = jnp.logical_or(jnp.logical_and(i == 1, pos == 0), jnp.logical_and(i == 9, pos == 3))
        open_face = jnp.where(rim, jnp.float32(0.0), jnp.float32(0.5))
        rows = Rows(lambda r: kx[i + 1, r], y0)
        for r in range(Q):
            kc, below, face, zface, total = rows.step(r)
            low = kc + kx[i, r]
            total = total + 0.5 * (low + (kc + kx[i + 2, r]))
            fx[i, r] = open_face * low
            fy[i, r] = face
            fz[i, r] = zface
            a0[i, r] = 1.0 / (inv0 + total)
            a1[i, r] = 1.0 / (inv1 + total)
        return carry

    lax.fori_loop(0, PLANES + 2, coef, 0)
    for r in range(Q):
        fx[10, r] = 0.5 * (kx[10, r] + kx[11, r])


def start_copies(src, planes, y0, buf, sems):
    out = []
    for i, p in enumerate(planes):
        out += lane_copies(src.at[p, pl.ds(y0, ROWS), :], lambda lane, i=i: buf.at[lane, i], sems.at[i])
    return out


def begin_start(prev, init, planes, y0, buf, sems):
    first = lax.axis_index("tm") == 0

    @pl.when(first)
    def _():
        for c in start_copies(init, planes, y0, buf, sems):
            c.start()

    @pl.when(jnp.logical_not(first))
    def _():
        for c in start_copies(prev, planes, y0, buf, sems):
            c.start()


def rim_kernel(where, at, *refs):
    n = len(where)
    zs, locs = refs[:n], refs[n : 2 * n]
    prev, init, rim, sa, sb, buf, sems = refs[2 * n :]
    even = lax.rem(lax.axis_index("space"), 2) == 0
    for i, y0 in enumerate(where):
        begin_start(prev, init, (0, 7), y0, buf.at[i], sems.at[i])
    for i, y0 in enumerate(where):
        for c in start_copies(prev, (0, 7), y0, buf.at[i], sems.at[i]):
            c.wait()
        for e in range(2):
            for r in range(Q):
                rim[2 * i + e, r] = rows_of(buf.at[i], e, r) + (locs[i][e, r] + zs[i][at[i][e], r])
    top = jnp.where(even, 1, 0)
    for i in range(n):
        for r in range(Q):
            sa[i, r] = rim[2 * i + top, r]
            sb[i, r] = rim[2 * i + 1 - top, r]


def sweep(src, rhs, a, fx, fy, fz, shift, count, store):
    G = 2

    def pair(t, carry):
        b = t * G
        uc = [src[b + g + 1, 0] for g in range(G)]
        last = [src[b + g + 1, Q - 1] for g in range(G)]
        flow = [sdown(fy[b + g + shift, Q - 1] * last[g]) for g in range(G)]
        for r in range(Q):
            low = src[b, r]
            high = src[b + G + 1, r]
            faces = [fx[b + g + shift, r] for g in range(G + 1)]
            column = [low] + uc + [high]
            nxt = []
            for g in range(G):
                un = src[b + g + 1, r + 1] if r < Q - 1 else sup(src[b + g + 1, 0])
                d = b + g + shift
                face = fy[d, r]
                zface = fz[d, r]
                n = faces[g] * column[g] + faces[g + 1] * column[g + 2]
                n = n + (flow[g] + face * un)
                n = n + (zface * znext(uc[g]) + zprev(zface * uc[g]))
                flow[g] = face * uc[g]
                store(b + g, r, rhs[d, r] + a[d, r] * n)
                nxt.append(un)
            uc = nxt
        return carry

    lax.fori_loop(0, count // G, pair, 0)


def two_sweeps(ub, mid, rhs, a, fx, fy, fz, store):
    def keep(d, r, value):
        mid[d, r] = value

    sweep(ub, rhs, a, fx, fy, fz, 0, PLANES + 2, keep)
    sweep(mid, rhs, a, fx, fy, fz, 1, PLANES, store)


def send_faces(u, sa, sb):
    even = lax.rem(lax.axis_index("space"), 2) == 0
    top = jnp.where(even, PLANES - 2, 0)

    def one(i, carry):
        sa[i] = u[top + i]
        sb[i] = u[PLANES - 2 - top + i]
        return carry

    lax.fori_loop(0, 2, one, 0)


def place_halo(ub, ha, hb):
    even = lax.rem(lax.axis_index("space"), 2) == 0

    def fill(low, high):
        for i in range(2):
            ub[i] = low[i]
            ub[10 + i] = high[i]

    @pl.when(even)
    def _():
        fill(hb, ha)

    @pl.when(jnp.logical_not(even))
    def _():
        fill(ha, hb)


def first_kernel(m, y0, slot, offset, z, loc, rim, ra, rb, a, fx, fy, fz, u0, prev, init, na, nb, fa, fb, rhs, u, sa, sb, ub, mid, buf, hbuf, fbuf, sems, hsems, fsems):
    node = lax.axis_index("node")
    even = lax.rem(lax.axis_index("space"), 2) == 0
    planes = tuple(range(1, PLANES - 1))
    begin_start(prev, init, planes, y0, buf, sems)
    begin_halos(na, nb, (1 + m,), y0, hbuf, hsems)
    begin_halos(fa, fb, (1 + m,), y0, fbuf, fsems)
    inv = inv_scale(m, node)

    def scaled(dst, src, at):
        for r in range(Q):
            dst[at, r] = src[r] * (a[at, r] * inv)

    @pl.when(even)
    def _():
        scaled(rhs, rb.at[slot], 0)
        scaled(rhs, ra.at[slot], 9)

    @pl.when(jnp.logical_not(even))
    def _():
        scaled(rhs, ra.at[slot], 0)
        scaled(rhs, rb.at[slot], 9)

    scaled(rhs, rim.at[2 * slot], 1)
    scaled(rhs, rim.at[2 * slot + 1], 8)

    def keep(p, carry):
        ub[p + 2] = u0[m * PLANES + p]
        return carry

    lax.fori_loop(0, PLANES, keep, 0)
    end_halos(na, nb, (1 + m,), y0, hbuf, hsems)
    end_halos(fa, fb, (1 + m,), y0, fbuf, fsems)

    def convert(i, carry):
        for r in range(Q):
            ub[1 + 9 * i, r] = rows_of(hbuf, i, r)
            ub[11 * i, r] = rows_of(fbuf, i, r)
        return carry

    lax.fori_loop(0, 2, convert, 0)
    for c in start_copies(prev, planes, y0, buf, sems):
        c.wait()

    def right(i, carry):
        for r in range(Q):
            rhs[i + 2, r] = (rows_of(buf, i, r) + (loc[i, r] + z[i + offset, r])) * (a[i + 2, r] * inv)
        return carry

    lax.fori_loop(0, PLANES - 2, right, 0)

    def store(d, r, value):
        u[d, r] = value

    two_sweeps(ub, mid, rhs, a, fx, fy, fz, store)
    send_faces(u, sa, sb)


def next_kernel(u, ha, hb, rhs, a, fx, fy, fz, unew, sa, sb, ub, mid):
    place_halo(ub, ha, hb)

    def keep(p, carry):
        ub[p + 2] = u[p]
        return carry

    lax.fori_loop(0, PLANES, keep, 0)

    def store(d, r, value):
        unew[d, r] = value

    two_sweeps(ub, mid, rhs, a, fx, fy, fz, store)
    send_faces(unew, sa, sb)


def last_kernel(m, part, aliased, u, ha, hb, rhs, a, fx, fy, fz, *rest):
    out, ub, mid, obuf, sems = rest[1:] if aliased else rest
    y0, first, kept = PARTS[part]
    place_halo(ub, ha, hb)

    def keep(p, carry):
        ub[p + 2] = u[p]
        return carry

    lax.fori_loop(0, PLANES, keep, 0)

    def store(d, r, value):
        for lane in range(2):
            obuf[lane, d, pl.ds(r, 8, stride=Q), :] = value[:, 128 * lane : 128 * lane + 128]

    two_sweeps(ub, mid, rhs, a, fx, fy, fz, store)
    cs = [
        pltpu.make_async_copy(
            obuf.at[lane, p, pl.ds(first, kept), :],
            out.at[0, m, p, pl.ds(y0 + first, kept), pl.ds(128 * lane, 128)],
            sems.at[lane, p],
        )
        for lane in range(2)
        for p in range(PLANES)
    ]
    for c in cs:
        c.start()
    for c in cs:
        c.wait()


DMA = pltpu.SemaphoreType.DMA
SWAP_A = [(0, 1), (1, 0), (2, 3), (3, 2)]
SWAP_B = [(1, 2), (2, 1)]


def to_a(x):
    return lax.ppermute(x, "space", SWAP_A)


def to_b(x):
    return lax.ppermute(x, "space", SWAP_B)


def swap_nodes(x):
    return lax.ppermute(x, "node", [(0, 1), (1, 0)])


def body(nodes, prev_final, u_init, cond):
    order = Order()
    plane_shape = lambda n: pltpu.VMEM((n, NY, NZ), F32)
    na, nb, fa, fb = order.call(
        "faces",
        faces_kernel,
        [(plane_shape(3), VM)] * 4,
        [(nodes, None), (cond, None)],
        [DMA((12,))],
        4,
        1.0,
    )
    na, nb, fa, fb = to_a(na), to_b(nb), to_a(fa), to_b(fb)
    half = lax.axis_size("tm") // 2
    blocks = 2 * half
    pairs = [
        (n * blocks + t, (1 - n if t == half - 1 else n) * blocks + t + 1)
        for n in range(2)
        for t in range(blocks - 1)
    ]
    prev = lax.ppermute(prev_final[0], ("node", "tm"), pairs)

    inner, edges, coef = [], [], {}
    for part, (y0, first, kept) in enumerate(PARTS):
        inner.append(
            order.call(
                "inner%d" % part,
                functools.partial(inner_kernel, y0, part, 1 - part),
                [(vshape(n), VM) for n in (2 * PLANES, PLANES, 8 if part else 6, 6 if part else 10, 6, 6)],
                [(nodes, None), (cond, None)],
                [pltpu.VMEM((2, 3 * PLANES, ROWS, 128), F32), DMA((PLANES, 3, 2))],
                12,
                5.0,
            )
        )
    def edge_step(part):
        y0 = PARTS[part][0]
        u0, kp = inner[part][:2]
        args = [(u0, True), (kp, True), (na, False), (nb, False)]
        if part:
            args += [(inner[1][2], True), (edges[0][1], True)]
        else:
            args += [(inner[0][3], True)]
        edges.append(
            order.call(
                "edge%d" % part,
                functools.partial(edge_kernel, y0, (0, 7) if part else (0, 1), (8, 9) if part else (0, 7)),
                [(vshape(8 if part else 2), VM), (vshape(10), VM), (vshape(2), VM), (vshape(2), VM)],
                args,
                [pltpu.VMEM((2, 6, ROWS, 128), F32), pltpu.VMEM((6, Q, 8, NZ), F32), DMA((6, 2))],
                8,
                2.5,
                {4: 0, 5: 1} if part else {4: 1},
                [prev, z_start] if part else [],
            )
        )

    def coef_step(part):
        coef[part] = order.call(
            "coef%d" % part,
            functools.partial(coef_kernel, PARTS[part][0]),
            [(vshape(11), VM)] + [(vshape(10), VM)] * 4,
            [(inner[part][1], True)] + [(x, False) for x in (na, nb, fa, fb)],
            [pltpu.VMEM((2, 2, ROWS, 128), F32)] * 2 + [pltpu.VMEM((12, Q, 8, NZ), F32), DMA((2, 2)), DMA((2, 2))],
            8,
            3.5,
        )

    z_start = swap_nodes(inner[0][2])
    edge_step(0)
    edge_step(1)
    coef_step(0)

    units = [(m, part) for m in range(2) for part in range(2)]
    z_inner = [z_start] + [swap_nodes(x) for x in (edges[1][0], edges[1][1], inner[1][3])]
    z_edge = [(swap_nodes(edges[0][0]), (0, 1)), (z_inner[1], (0, 7)), (z_inner[2], (0, 7)), (z_inner[2], (8, 9))]
    state = {}
    out = [None]

    def coefs(unit):
        m, part = units[unit]
        return [(x, True) for x in [coef[part][3 + m]] + coef[part][:3]]

    def rim_step(which):
        n = len(which)
        parts = [units[unit][1] for unit in which]
        rim, ra, rb = order.call(
            "rim%d" % which[0],
            functools.partial(rim_kernel, tuple(PARTS[part][0] for part in parts), tuple(z_edge[unit][1] for unit in which)),
            [(vshape(2 * n), VM), (vshape(n), VM), (vshape(n), VM)],
            [(z_edge[unit][0], True) for unit in which]
            + [(edges[units[unit][1]][2 + units[unit][0]], True) for unit in which]
            + [(prev, False), (u_init, False)],
            [pltpu.VMEM((n, 2, 2, ROWS, 128), F32), DMA((n, 2, 2))],
            4,
            0.5,
        )
        ra, rb = to_a(ra), to_b(rb)
        for slot, unit in enumerate(which):
            state[unit] = (slot, rim, ra, rb)

    def first_step(unit):
        m, part = units[unit]
        slot, rim, ra, rb = state[unit]
        rhs, u, sa, sb = order.call(
            "first%d" % unit,
            functools.partial(first_kernel, m, PARTS[part][0], slot, 1 if unit in (1, 2) else 0),
            [(vshape(10), VM), (vshape(8), VM), (vshape(2), VM), (vshape(2), VM)],
            [(x, True) for x in (z_inner[unit], inner[part][4 + m], rim, ra, rb)]
            + coefs(unit)
            + [(inner[part][0], True)]
            + [(x, False) for x in (prev, u_init, na, nb, fa, fb)],
            [
                pltpu.VMEM((12, Q, 8, NZ), F32),
                pltpu.VMEM((10, Q, 8, NZ), F32),
                pltpu.VMEM((2, 6, ROWS, 128), F32),
                pltpu.VMEM((2, 2, ROWS, 128), F32),
                pltpu.VMEM((2, 2, ROWS, 128), F32),
                DMA((6, 2)),
                DMA((2, 2)),
                DMA((2, 2)),
            ],
            12,
            3.0,
        )
        state[unit] = (rhs, u, to_a(sa), to_b(sb))

    def next_step(unit, index):
        rhs, u, ha, hb = state[unit]
        u, sa, sb = order.call(
            "next%d_%d" % (unit, index),
            next_kernel,
            [(vshape(8), VM), (vshape(2), VM), (vshape(2), VM)],
            [(x, True) for x in (u, ha, hb, rhs)] + coefs(unit),
            [pltpu.VMEM((12, Q, 8, NZ), F32), pltpu.VMEM((10, Q, 8, NZ), F32)],
            8,
            2.5,
        )
        state[unit] = (rhs, u, to_a(sa), to_b(sb))

    def last_step(unit):
        m, part = units[unit]
        rhs, u, ha, hb = state[unit]
        args = [(x, True) for x in (u, ha, hb, rhs)] + coefs(unit)
        aliased = out[0] is not None
        if aliased:
            args.append((out[0], False))
        (out[0],) = order.call(
            "last%d" % unit,
            functools.partial(last_kernel, m, part, aliased),
            [((1, 2, PLANES, NY, NZ), ANY)],
            args,
            [
                pltpu.VMEM((12, Q, 8, NZ), F32),
                pltpu.VMEM((10, Q, 8, NZ), F32),
                pltpu.VMEM((2, 8, ROWS, 128), F32),
                DMA((2, 8)),
            ],
            8,
            3.5,
            {8: 0} if aliased else None,
        )

    C, R, S, N, M, L = range(6)
    plan = (
        (R, 0), (C, 1), (S, 0), (N, 0), (R, 1), (M, 0), (S, 1), (L, 0), (N, 1), (R, 2),
        (M, 1), (S, 2), (L, 1), (S, 3), (N, 2), (N, 3), (M, 2), (M, 3), (L, 2), (L, 3),
    )
    for kind, unit in plan:
        if kind == C:
            coef_step(unit)
        elif kind == R:
            rim_step((2, 3) if unit == 2 else (unit,))
        elif kind == S:
            first_step(unit)
        elif kind == L:
            last_step(unit)
        else:
            next_step(unit, kind)
    return out[0]


def solution(mesh):
    in_specs = (
        P("tm", "node", "space", None, None),
        P("tm", "space", None, None),
        P("space", None, None),
        P("space", None, None),
    )
    out_specs = P("tm", "node", "space", None, None)
    return jax.shard_map(body, mesh=mesh, in_specs=in_specs, out_specs=out_specs, check_vma=False)
```

```python
import functools

import jax
import jax.numpy as jnp
from jax import lax
from jax.experimental import pallas as pl
from jax.experimental.pallas import tpu as pltpu
from jax.sharding import PartitionSpec as P

radau_points = [0.08858795951270394, 0.4094668644407347, 0.787659461760847, 1.0]

Q = 17
ROWS = 8 * Q
PARTS = ((0, 0, 128), (120, 8, 128))
NY = 256
NZ = 256
PLANES = 8
F32 = jnp.float32


def mixing_table():
    count_nodes = len(radau_points)
    table = [[0.0] * count_nodes for row_index in range(count_nodes)]
    for column in range(count_nodes):
        coefs = [1.0]
        for other in range(count_nodes):
            if other != column:
                scale = 1.0 / (radau_points[column] - radau_points[other])
                shifted = [0.0] + coefs
                lowered = [value * radau_points[other] for value in coefs] + [0.0]
                coefs = [(shifted[k] - lowered[k]) * scale for k in range(len(shifted))]
        for row_index in range(count_nodes):
            point = radau_points[row_index]
            integral = 0.0
            for power in range(len(coefs)):
                integral = integral + coefs[power] * point ** (power + 1) / (power + 1)
            table[row_index][column] = integral
        table[column][column] = table[column][column] - radau_points[column]
    return table


WEIGHTS = mixing_table()

ANY = pl.BlockSpec(memory_space=pl.ANY)
VM = pl.BlockSpec(memory_space=pltpu.VMEM)


def vshape(planes):
    return pltpu.VMEM((planes, Q, 8, NZ), F32)


HB = pl.BlockSpec(memory_space=pltpu.HBM)


def pin(x):
    return pltpu.with_memory_space_constraint(x, pltpu.VMEM)


def place(x, where):
    if where is False:
        return x
    return pin(x) if where else pltpu.with_memory_space_constraint(x, pltpu.HBM)


TOKEN = pltpu.VMEM((8, 128), F32)


def with_token(kernel):
    def run(before, *refs):
        ins = refs[: run.ins]
        rest = refs[run.ins + run.skip :]
        rest[run.outs][...] = before[...]
        kernel(*ins, *rest[: run.outs], *rest[run.outs + 1 :])

    return run


class Order:
    def __init__(self):
        self.token = jnp.zeros((8, 128), F32)

    def call(self, name, kernel, outs, ins, scratch, limit_mib, us, aliases=None, after=()):
        run = with_token(kernel)
        run.ins, run.outs, run.skip = len(ins), len(outs), len(after)
        ins = ins + [(a, False) for a in after]
        operands = [pin(self.token)] + [place(a, where) for a, where in ins]
        *results, self.token = pl.pallas_call(
            run,
            out_shape=[o if s is VM else jax.ShapeDtypeStruct(o, F32) for o, s in outs] + [TOKEN],
            in_specs=[VM] + [{True: VM, None: HB, False: ANY}[where] for a, where in ins],
            out_specs=[s for o, s in outs] + [VM],
            scratch_shapes=scratch,
            input_output_aliases={k + 1: v for k, v in (aliases or {}).items()},
            compiler_params=pltpu.CompilerParams(vmem_limit_bytes=limit_mib << 20),
            cost_estimate=pl.CostEstimate(flops=int(us * FLOPS), bytes_accessed=0, transcendentals=0),
            name=name,
        )(*operands)
        return results


FLOPS = 7e8


def zprev(v):
    return pltpu.roll(v, 1, axis=1)


def znext(v):
    return pltpu.roll(v, NZ - 1, axis=1)


def sdown(v):
    return pltpu.roll(v, 1, axis=0)


def sup(v):
    return pltpu.roll(v, 7, axis=0)


def rows_of(buf, plane, r):
    return jnp.concatenate([buf[lane, plane, pl.ds(r, 8, stride=Q), :] for lane in range(2)], axis=-1)


def lane_copies(src_plane, dst_plane, sems):
    return [
        pltpu.make_async_copy(src_plane.at[:, pl.ds(128 * lane, 128)], dst_plane(lane), sems.at[lane])
        for lane in range(2)
    ]


def pick(table_low, table_high, node):
    return jnp.where(node == 0, jnp.float32(table_low), jnp.float32(table_high))


def own_scale(m, node):
    return pick(radau_points[m], radau_points[2 + m], node)


def inv_scale(m, node):
    return pick(1.0 / radau_points[m], 1.0 / radau_points[2 + m], node)


def weights_for(node):
    remote = [[pick(WEIGHTS[2 + m][j], WEIGHTS[m][2 + j], node) for j in range(2)] for m in range(2)]
    local = [[pick(WEIGHTS[m][j], WEIGHTS[2 + m][2 + j], node) for j in range(2)] for m in range(2)]
    return remote, local


class Rows:
    def __init__(self, k_at, y0):
        self.k_at = k_at
        self.first = y0 == 0
        self.last = y0 + ROWS == NY
        sub = lax.broadcasted_iota(jnp.int32, (8, NZ), 0)
        lane = lax.broadcasted_iota(jnp.int32, (8, NZ), 1)
        self.top = sub == 0
        self.bottom = sub == 7
        self.left = lane == 0
        self.right = lane == NZ - 1
        kc = k_at(0)
        kb = sdown(k_at(Q - 1))
        face = 0.5 * (kb + kc)
        if self.first:
            self.prev_sum = jnp.where(self.top, kc, face)
            self.prev = jnp.where(self.top, 0.0, face)
        else:
            self.prev_sum = face
            self.prev = face
        self.kc = kc

    def step(self, r):
        kc = self.kc
        kn = self.k_at(r + 1) if r < Q - 1 else sup(self.k_at(0))
        face = 0.5 * (kc + kn)
        face_sum = face
        if r == Q - 1:
            if self.last:
                face_sum = jnp.where(self.bottom, kc, face)
            face = jnp.where(self.bottom, 0.0, face)
        zface = 0.5 * (kc + znext(kc))
        zsum = jnp.where(self.right, kc, zface) + jnp.where(self.left, kc, zprev(zface))
        zface = jnp.where(self.right, 0.0, zface)
        total = self.prev_sum + face_sum + zsum
        below = self.prev
        self.prev = face
        self.prev_sum = face_sum
        self.kc = kn
        return kc, below, face, zface, total


def flux_rows(k_at, k_low, k_up, us, u_low, u_up, y0, emit):
    rows = Rows(k_at, y0)
    state = [(u(0), sdown(u(Q - 1))) for u in us]
    for r in range(Q):
        kc, below, face, zface, total = rows.step(r)
        fxl = 0.5 * (kc + k_low(r))
        fxu = 0.5 * (kc + k_up(r))
        total = total + (fxl + fxu)
        fluxes = []
        for j in range(2):
            uc, ub = state[j]
            un = us[j](r + 1) if r < Q - 1 else sup(us[j](0))
            n = fxl * u_low[j](r) + fxu * u_up[j](r)
            n = n + below * ub + face * un
            n = n + zface * znext(uc) + zprev(zface * uc)
            fluxes.append(n - total * uc)
            state[j] = (un, uc)
        emit(r, fluxes)


def inner_kernel(y0, offset0, offset1, nodes, cond, u0, kp, rem0, rem1, loc0, loc1, buf, sems):
    node = lax.axis_index("node")
    remote, local = weights_for(node)
    sources = [nodes.at[0, 0], nodes.at[0, 1], cond]

    def copies(p):
        out = []
        for a in range(3):
            out += lane_copies(
                sources[a].at[p, pl.ds(y0, ROWS), :], lambda lane, a=a: buf.at[lane, 3 * p + a], sems.at[p, a]
            )
        return out

    for p in range(PLANES):
        for c in copies(p):
            c.start()

    def convert(p, carry):
        for c in copies(p):
            c.wait()
        for r in range(Q):
            u0[p, r] = rows_of(buf, 3 * p, r)
            u0[PLANES + p, r] = rows_of(buf, 3 * p + 1, r)
            kp[p, r] = rows_of(buf, 3 * p + 2, r)
        return carry

    lax.fori_loop(0, 2, convert, 0)

    def plane(i, carry):
        p = i + 1
        convert(p + 1, carry)

        def emit(r, f):
            rem0[i + offset0, r] = remote[0][0] * f[0] + remote[0][1] * f[1]
            rem1[i + offset1, r] = remote[1][0] * f[0] + remote[1][1] * f[1]
            loc0[i, r] = local[0][0] * f[0] + local[0][1] * f[1]
            loc1[i, r] = local[1][0] * f[0] + local[1][1] * f[1]

        at = lambda j, d: (lambda r: u0[j * PLANES + p + d, r])
        flux_rows(
            lambda r: kp[p, r],
            lambda r: kp[p - 1, r],
            lambda r: kp[p + 1, r],
            [at(0, 0), at(1, 0)],
            [at(0, -1), at(1, -1)],
            [at(0, 1), at(1, 1)],
            y0,
            emit,
        )
        return carry

    lax.fori_loop(0, PLANES - 2, plane, 0)


def faces_kernel(depth, nodes, cond, sa, sb, sems):
    even = lax.rem(lax.axis_index("space"), 2) == 0

    def copies(high, low):
        pairs = []
        for dst, p in ((high, PLANES - 1 - depth), (low, depth)):
            pairs += [(cond.at[p], dst.at[0])] + [(nodes.at[0, j, p], dst.at[1 + j]) for j in range(2)]
        return [pltpu.make_async_copy(src, dst, sems.at[i]) for i, (src, dst) in enumerate(pairs)]

    @pl.when(even)
    def _():
        for c in copies(sa, sb):
            c.start()

    @pl.when(jnp.logical_not(even))
    def _():
        for c in copies(sb, sa):
            c.start()

    for c in copies(sa, sb):
        c.wait()


def halo_copies(near, planes, y0, buf, base, sems):
    out = []
    for i, p in enumerate(planes):
        out += lane_copies(
            near.at[p, pl.ds(y0, ROWS), :], lambda lane, i=i: buf.at[lane, base + i], sems.at[base + i]
        )
    return out


def begin_halos(na, nb, planes, y0, buf, sems):
    even = lax.rem(lax.axis_index("space"), 2) == 0
    n = len(planes)

    @pl.when(even)
    def _():
        for c in halo_copies(nb, planes, y0, buf, 0, sems) + halo_copies(na, planes, y0, buf, n, sems):
            c.start()

    @pl.when(jnp.logical_not(even))
    def _():
        for c in halo_copies(na, planes, y0, buf, 0, sems) + halo_copies(nb, planes, y0, buf, n, sems):
            c.start()


def end_halos(na, nb, planes, y0, buf, sems):
    for c in halo_copies(na, planes, y0, buf, 0, sems) + halo_copies(nb, planes, y0, buf, len(planes), sems):
        c.wait()


def edge_kernel(y0, at0, at1, u0, kp, na, nb, *refs):
    rem0, rem1, loc0, loc1, buf, hu, sems = refs[-7:]
    node = lax.axis_index("node")
    pos = lax.axis_index("space")
    remote, local = weights_for(node)
    planes = (0, 1, 2)
    begin_halos(na, nb, planes, y0, buf, sems)
    end_halos(na, nb, planes, y0, buf, sems)

    def convert(i, carry):
        for r in range(Q):
            hu[i, r] = rows_of(buf, i, r)
        return carry

    lax.fori_loop(0, 6, convert, 0)

    @pl.when(pos == 0)
    def _():
        hu[0] = kp[0]

    @pl.when(pos == 3)
    def _():
        hu[3] = kp[PLANES - 1]

    for e in range(2):
        p = 7 * e

        def emit(r, f, e=e):
            rem0[at0[e], r] = remote[0][0] * f[0] + remote[0][1] * f[1]
            rem1[at1[e], r] = remote[1][0] * f[0] + remote[1][1] * f[1]
            loc0[e, r] = local[0][0] * f[0] + local[0][1] * f[1]
            loc1[e, r] = local[1][0] * f[0] + local[1][1] * f[1]

        at = lambda j, d, p=p: (lambda r: u0[j * PLANES + p + d, r])
        kat = lambda d, p=p: (lambda r: kp[p + d, r])
        halo = lambda i, e=e: (lambda r: hu[3 * e + i, r])
        flux_rows(
            kat(0),
            kat(-1) if e else halo(0),
            halo(0) if e else kat(1),
            [at(0, 0), at(1, 0)],
            [at(0, -1), at(1, -1)] if e else [halo(1), halo(2)],
            [halo(1), halo(2)] if e else [at(0, 1), at(1, 1)],
            y0,
            emit,
        )


def coef_kernel(y0, kp, na, nb, fa, fb, fx, fy, fz, a0, a1, buf, far, kx, sems, far_sems):
    node = lax.axis_index("node")
    pos = lax.axis_index("space")
    begin_halos(na, nb, (0,), y0, buf, sems)
    begin_halos(fa, fb, (0,), y0, far, far_sems)

    def keep(p, carry):
        kx[p + 2] = kp[p]
        return carry

    lax.fori_loop(0, PLANES, keep, 0)
    end_halos(na, nb, (0,), y0, buf, sems)
    end_halos(fa, fb, (0,), y0, far, far_sems)

    @pl.when(pos > 0)
    def _():
        for r in range(Q):
            kx[0, r] = rows_of(far, 0, r)
            kx[1, r] = rows_of(buf, 0, r)

    @pl.when(pos == 0)
    def _():
        kx[0] = kp[0]
        kx[1] = kp[0]

    @pl.when(pos < 3)
    def _():
        for r in range(Q):
            kx[10, r] = rows_of(buf, 1, r)
            kx[11, r] = rows_of(far, 1, r)

    @pl.when(pos == 3)
    def _():
        kx[10] = kp[7]
        kx[11] = kp[7]

    inv0, inv1 = inv_scale(0, node), inv_scale(1, node)

    def coef(i, carry):
        rim = jnp.logical_or(jnp.logical_and(i == 1, pos == 0), jnp.logical_and(i == 9, pos == 3))
        open_face = jnp.where(rim, jnp.float32(0.0), jnp.float32(0.5))
        rows = Rows(lambda r: kx[i + 1, r], y0)
        for r in range(Q):
            kc, below, face, zface, total = rows.step(r)
            low = kc + kx[i, r]
            total = total + 0.5 * (low + (kc + kx[i + 2, r]))
            fx[i, r] = open_face * low
            fy[i, r] = face
            fz[i, r] = zface
            a0[i, r] = 1.0 / (inv0 + total)
            a1[i, r] = 1.0 / (inv1 + total)
        return carry

    lax.fori_loop(0, PLANES + 2, coef, 0)
    for r in range(Q):
        fx[10, r] = 0.5 * (kx[10, r] + kx[11, r])


def start_copies(src, planes, y0, buf, sems):
    out = []
    for i, p in enumerate(planes):
        out += lane_copies(src.at[p, pl.ds(y0, ROWS), :], lambda lane, i=i: buf.at[lane, i], sems.at[i])
    return out


def begin_start(prev, init, planes, y0, buf, sems):
    first = lax.axis_index("tm") == 0

    @pl.when(first)
    def _():
        for c in start_copies(init, planes, y0, buf, sems):
            c.start()

    @pl.when(jnp.logical_not(first))
    def _():
        for c in start_copies(prev, planes, y0, buf, sems):
            c.start()


def rim_kernel(where, at, *refs):
    n = len(where)
    zs, locs = refs[:n], refs[n : 2 * n]
    prev, init, rim, sa, sb, buf, sems = refs[2 * n :]
    even = lax.rem(lax.axis_index("space"), 2) == 0
    for i, y0 in enumerate(where):
        begin_start(prev, init, (0, 7), y0, buf.at[i], sems.at[i])
    for i, y0 in enumerate(where):
        for c in start_copies(prev, (0, 7), y0, buf.at[i], sems.at[i]):
            c.wait()
        for e in range(2):
            for r in range(Q):
                rim[2 * i + e, r] = rows_of(buf.at[i], e, r) + (locs[i][e, r] + zs[i][at[i][e], r])
    top = jnp.where(even, 1, 0)
    for i in range(n):
        for r in range(Q):
            sa[i, r] = rim[2 * i + top, r]
            sb[i, r] = rim[2 * i + 1 - top, r]


def sweep(src, rhs, a, fx, fy, fz, shift, count, store):
    G = 2

    def pair(t, carry):
        b = t * G
        uc = [src[b + g + 1, 0] for g in range(G)]
        last = [src[b + g + 1, Q - 1] for g in range(G)]
        flow = [sdown(fy[b + g + shift, Q - 1] * last[g]) for g in range(G)]
        for r in range(Q):
            low = src[b, r]
            high = src[b + G + 1, r]
            faces = [fx[b + g + shift, r] for g in range(G + 1)]
            column = [low] + uc + [high]
            nxt = []
            for g in range(G):
                un = src[b + g + 1, r + 1] if r < Q - 1 else sup(src[b + g + 1, 0])
                d = b + g + shift
                face = fy[d, r]
                zface = fz[d, r]
                n = faces[g] * column[g] + faces[g + 1] * column[g + 2]
                n = n + (flow[g] + face * un)
                n = n + (zface * znext(uc[g]) + zprev(zface * uc[g]))
                flow[g] = face * uc[g]
                store(b + g, r, rhs[d, r] + a[d, r] * n)
                nxt.append(un)
            uc = nxt
        return carry

    lax.fori_loop(0, count // G, pair, 0)


def two_sweeps(ub, mid, rhs, a, fx, fy, fz, store):
    def keep(d, r, value):
        mid[d, r] = value

    sweep(ub, rhs, a, fx, fy, fz, 0, PLANES + 2, keep)
    sweep(mid, rhs, a, fx, fy, fz, 1, PLANES, store)


def send_faces(u, sa, sb):
    even = lax.rem(lax.axis_index("space"), 2) == 0
    top = jnp.where(even, PLANES - 2, 0)

    def one(i, carry):
        sa[i] = u[top + i]
        sb[i] = u[PLANES - 2 - top + i]
        return carry

    lax.fori_loop(0, 2, one, 0)


def place_halo(ub, ha, hb):
    even = lax.rem(lax.axis_index("space"), 2) == 0

    def fill(low, high):
        for i in range(2):
            ub[i] = low[i]
            ub[10 + i] = high[i]

    @pl.when(even)
    def _():
        fill(hb, ha)

    @pl.when(jnp.logical_not(even))
    def _():
        fill(ha, hb)


def first_kernel(m, y0, slot, offset, z, loc, rim, ra, rb, a, fx, fy, fz, u0, prev, init, na, nb, fa, fb, rhs, u, sa, sb, ub, mid, buf, hbuf, fbuf, sems, hsems, fsems):
    node = lax.axis_index("node")
    even = lax.rem(lax.axis_index("space"), 2) == 0
    planes = tuple(range(1, PLANES - 1))
    begin_start(prev, init, planes, y0, buf, sems)
    begin_halos(na, nb, (1 + m,), y0, hbuf, hsems)
    begin_halos(fa, fb, (1 + m,), y0, fbuf, fsems)
    inv = inv_scale(m, node)

    def scaled(dst, src, at):
        for r in range(Q):
            dst[at, r] = src[r] * (a[at, r] * inv)

    @pl.when(even)
    def _():
        scaled(rhs, rb.at[slot], 0)
        scaled(rhs, ra.at[slot], 9)

    @pl.when(jnp.logical_not(even))
    def _():
        scaled(rhs, ra.at[slot], 0)
        scaled(rhs, rb.at[slot], 9)

    scaled(rhs, rim.at[2 * slot], 1)
    scaled(rhs, rim.at[2 * slot + 1], 8)

    def keep(p, carry):
        ub[p + 2] = u0[m * PLANES + p]
        return carry

    lax.fori_loop(0, PLANES, keep, 0)
    end_halos(na, nb, (1 + m,), y0, hbuf, hsems)
    end_halos(fa, fb, (1 + m,), y0, fbuf, fsems)

    def convert(i, carry):
        for r in range(Q):
            ub[1 + 9 * i, r] = rows_of(hbuf, i, r)
            ub[11 * i, r] = rows_of(fbuf, i, r)
        return carry

    lax.fori_loop(0, 2, convert, 0)
    for c in start_copies(prev, planes, y0, buf, sems):
        c.wait()

    def right(i, carry):
        for r in range(Q):
            rhs[i + 2, r] = (rows_of(buf, i, r) + (loc[i, r] + z[i + offset, r])) * (a[i + 2, r] * inv)
        return carry

    lax.fori_loop(0, PLANES - 2, right, 0)

    def store(d, r, value):
        u[d, r] = value

    two_sweeps(ub, mid, rhs, a, fx, fy, fz, store)
    send_faces(u, sa, sb)


def next_kernel(u, ha, hb, rhs, a, fx, fy, fz, unew, sa, sb, ub, mid):
    place_halo(ub, ha, hb)

    def keep(p, carry):
        ub[p + 2] = u[p]
        return carry

    lax.fori_loop(0, PLANES, keep, 0)

    def store(d, r, value):
        unew[d, r] = value

    two_sweeps(ub, mid, rhs, a, fx, fy, fz, store)
    send_faces(unew, sa, sb)


def last_kernel(m, part, aliased, u, ha, hb, rhs, a, fx, fy, fz, *rest):
    out, ub, mid, obuf, sems = rest[1:] if aliased else rest
    y0, first, kept = PARTS[part]
    place_halo(ub, ha, hb)

    def keep(p, carry):
        ub[p + 2] = u[p]
        return carry

    lax.fori_loop(0, PLANES, keep, 0)

    def store(d, r, value):
        for lane in range(2):
            obuf[lane, d, pl.ds(r, 8, stride=Q), :] = value[:, 128 * lane : 128 * lane + 128]

    two_sweeps(ub, mid, rhs, a, fx, fy, fz, store)
    cs = [
        pltpu.make_async_copy(
            obuf.at[lane, p, pl.ds(first, kept), :],
            out.at[0, m, p, pl.ds(y0 + first, kept), pl.ds(128 * lane, 128)],
            sems.at[lane, p],
        )
        for lane in range(2)
        for p in range(PLANES)
    ]
    for c in cs:
        c.start()
    for c in cs:
        c.wait()


DMA = pltpu.SemaphoreType.DMA
SWAP_A = [(0, 1), (1, 0), (2, 3), (3, 2)]
SWAP_B = [(1, 2), (2, 1)]


def to_a(x):
    return lax.ppermute(x, "space", SWAP_A)


def to_b(x):
    return lax.ppermute(x, "space", SWAP_B)


def swap_nodes(x):
    return lax.ppermute(x, "node", [(0, 1), (1, 0)])


def body(nodes, prev_final, u_init, cond):
    order = Order()

    def faces(depth):
        sa, sb = order.call(
            "faces%d" % depth,
            functools.partial(faces_kernel, depth),
            [(pltpu.VMEM((3, NY, NZ), F32), VM)] * 2,
            [(nodes, None), (cond, None)],
            [DMA((6,))],
            4,
            0.7,
        )
        return to_a(sa), to_b(sb)

    na, nb = faces(0)
    half = lax.axis_size("tm") // 2
    blocks = 2 * half
    pairs = [
        (n * blocks + t, (1 - n if t == half - 1 else n) * blocks + t + 1)
        for n in range(2)
        for t in range(blocks - 1)
    ]
    prev = lax.ppermute(prev_final[0], ("node", "tm"), pairs)

    inner, edges, coef = [], [], {}
    for part, (y0, first, kept) in enumerate(PARTS):
        inner.append(
            order.call(
                "inner%d" % part,
                functools.partial(inner_kernel, y0, part, 1 - part),
                [(vshape(n), VM) for n in (2 * PLANES, PLANES, 8 if part else 6, 6 if part else 10, 6, 6)],
                [(nodes, None), (cond, None)],
                [pltpu.VMEM((2, 3 * PLANES, ROWS, 128), F32), DMA((PLANES, 3, 2))],
                12,
                5.0,
            )
        )
    def edge_step(part):
        y0 = PARTS[part][0]
        u0, kp = inner[part][:2]
        args = [(u0, True), (kp, True), (na, False), (nb, False)]
        if part:
            args += [(inner[1][2], True), (edges[0][1], True)]
        else:
            args += [(inner[0][3], True)]
        edges.append(
            order.call(
                "edge%d" % part,
                functools.partial(edge_kernel, y0, (0, 7) if part else (0, 1), (8, 9) if part else (0, 7)),
                [(vshape(8 if part else 2), VM), (vshape(10), VM), (vshape(2), VM), (vshape(2), VM)],
                args,
                [pltpu.VMEM((2, 6, ROWS, 128), F32), pltpu.VMEM((6, Q, 8, NZ), F32), DMA((6, 2))],
                8,
                2.5,
                {4: 0, 5: 1} if part else {4: 1},
                [prev, z_start] if part else [],
            )
        )

    def coef_step(part):
        coef[part] = order.call(
            "coef%d" % part,
            functools.partial(coef_kernel, PARTS[part][0]),
            [(vshape(11), VM)] + [(vshape(10), VM)] * 4,
            [(inner[part][1], True)] + [(x, False) for x in (na, nb, fa, fb)],
            [pltpu.VMEM((2, 2, ROWS, 128), F32)] * 2 + [pltpu.VMEM((12, Q, 8, NZ), F32), DMA((2, 2)), DMA((2, 2))],
            8,
            3.5,
        )

    fa, fb = faces(1)
    z_start = swap_nodes(inner[0][2])
    edge_step(0)
    edge_step(1)

    units = [(m, part) for m in range(2) for part in range(2)]
    z_inner = [z_start] + [swap_nodes(x) for x in (edges[1][0], edges[1][1], inner[1][3])]
    z_edge = [(swap_nodes(edges[0][0]), (0, 1)), (z_inner[1], (0, 7)), (z_inner[2], (0, 7)), (z_inner[2], (8, 9))]
    state = {}
    out = [None]

    def coefs(unit):
        m, part = units[unit]
        return [(x, True) for x in [coef[part][3 + m]] + coef[part][:3]]

    def rim_step(which):
        n = len(which)
        parts = [units[unit][1] for unit in which]
        rim, ra, rb = order.call(
            "rim%d" % which[0],
            functools.partial(rim_kernel, tuple(PARTS[part][0] for part in parts), tuple(z_edge[unit][1] for unit in which)),
            [(vshape(2 * n), VM), (vshape(n), VM), (vshape(n), VM)],
            [(z_edge[unit][0], True) for unit in which]
            + [(edges[units[unit][1]][2 + units[unit][0]], True) for unit in which]
            + [(prev, False), (u_init, False)],
            [pltpu.VMEM((n, 2, 2, ROWS, 128), F32), DMA((n, 2, 2))],
            4,
            0.5,
        )
        ra, rb = to_a(ra), to_b(rb)
        for slot, unit in enumerate(which):
            state[unit] = (slot, rim, ra, rb)

    def first_step(unit):
        m, part = units[unit]
        slot, rim, ra, rb = state[unit]
        rhs, u, sa, sb = order.call(
            "first%d" % unit,
            functools.partial(first_kernel, m, PARTS[part][0], slot, 1 if unit in (1, 2) else 0),
            [(vshape(10), VM), (vshape(8), VM), (vshape(2), VM), (vshape(2), VM)],
            [(x, True) for x in (z_inner[unit], inner[part][4 + m], rim, ra, rb)]
            + coefs(unit)
            + [(inner[part][0], True)]
            + [(x, False) for x in (prev, u_init, na, nb, fa, fb)],
            [
                pltpu.VMEM((12, Q, 8, NZ), F32),
                pltpu.VMEM((10, Q, 8, NZ), F32),
                pltpu.VMEM((2, 6, ROWS, 128), F32),
                pltpu.VMEM((2, 2, ROWS, 128), F32),
                pltpu.VMEM((2, 2, ROWS, 128), F32),
                DMA((6, 2)),
                DMA((2, 2)),
                DMA((2, 2)),
            ],
            12,
            3.0,
        )
        state[unit] = (rhs, u, to_a(sa), to_b(sb))

    def next_step(unit, index):
        rhs, u, ha, hb = state[unit]
        u, sa, sb = order.call(
            "next%d_%d" % (unit, index),
            next_kernel,
            [(vshape(8), VM), (vshape(2), VM), (vshape(2), VM)],
            [(x, True) for x in (u, ha, hb, rhs)] + coefs(unit),
            [pltpu.VMEM((12, Q, 8, NZ), F32), pltpu.VMEM((10, Q, 8, NZ), F32)],
            8,
            2.5,
        )
        state[unit] = (rhs, u, to_a(sa), to_b(sb))

    def last_step(unit):
        m, part = units[unit]
        rhs, u, ha, hb = state[unit]
        args = [(x, True) for x in (u, ha, hb, rhs)] + coefs(unit)
        aliased = out[0] is not None
        if aliased:
            args.append((out[0], False))
        (out[0],) = order.call(
            "last%d" % unit,
            functools.partial(last_kernel, m, part, aliased),
            [((1, 2, PLANES, NY, NZ), ANY)],
            args,
            [
                pltpu.VMEM((12, Q, 8, NZ), F32),
                pltpu.VMEM((10, Q, 8, NZ), F32),
                pltpu.VMEM((2, 8, ROWS, 128), F32),
                DMA((2, 8)),
            ],
            8,
            3.5,
            {8: 0} if aliased else None,
        )

    C, R, S, N, M, L = range(6)
    plan = (
        (R, 0), (C, 0), (C, 1), (S, 0), (N, 0), (R, 1), (M, 0), (S, 1), (L, 0), (N, 1), (R, 2),
        (M, 1), (S, 2), (L, 1), (S, 3), (N, 2), (N, 3), (M, 2), (M, 3), (L, 2), (L, 3),
    )
    for kind, unit in plan:
        if kind == C:
            coef_step(unit)
        elif kind == R:
            rim_step((2, 3) if unit == 2 else (unit,))
        elif kind == S:
            first_step(unit)
        elif kind == L:
            last_step(unit)
        else:
            next_step(unit, kind)
    return out[0]


def solution(mesh):
    in_specs = (
        P("tm", "node", "space", None, None),
        P("tm", "space", None, None),
        P("space", None, None),
        P("space", None, None),
    )
    out_specs = P("tm", "node", "space", None, None)
    return jax.shard_map(body, mesh=mesh, in_specs=in_specs, out_specs=out_specs, check_vma=False)
```

```python
import functools

import jax
import jax.numpy as jnp
from jax import lax
from jax.experimental import pallas as pl
from jax.experimental.pallas import tpu as pltpu
from jax.sharding import PartitionSpec as P

radau_points = [0.08858795951270394, 0.4094668644407347, 0.787659461760847, 1.0]

Q = 17
ROWS = 8 * Q
PARTS = ((0, 0, 128), (120, 8, 128))
NY = 256
NZ = 256
PLANES = 8
F32 = jnp.float32


def mixing_table():
    count_nodes = len(radau_points)
    table = [[0.0] * count_nodes for row_index in range(count_nodes)]
    for column in range(count_nodes):
        coefs = [1.0]
        for other in range(count_nodes):
            if other != column:
                scale = 1.0 / (radau_points[column] - radau_points[other])
                shifted = [0.0] + coefs
                lowered = [value * radau_points[other] for value in coefs] + [0.0]
                coefs = [(shifted[k] - lowered[k]) * scale for k in range(len(shifted))]
        for row_index in range(count_nodes):
            point = radau_points[row_index]
            integral = 0.0
            for power in range(len(coefs)):
                integral = integral + coefs[power] * point ** (power + 1) / (power + 1)
            table[row_index][column] = integral
        table[column][column] = table[column][column] - radau_points[column]
    return table


WEIGHTS = mixing_table()

ANY = pl.BlockSpec(memory_space=pl.ANY)
VM = pl.BlockSpec(memory_space=pltpu.VMEM)


def vshape(planes):
    return pltpu.VMEM((planes, Q, 8, NZ), F32)


HB = pl.BlockSpec(memory_space=pltpu.HBM)


def pin(x):
    return pltpu.with_memory_space_constraint(x, pltpu.VMEM)


def place(x, where):
    if where is False:
        return x
    return pin(x) if where else pltpu.with_memory_space_constraint(x, pltpu.HBM)


TOKEN = pltpu.VMEM((8, 128), F32)


def with_token(kernel):
    def run(before, *refs):
        ins = refs[: run.ins]
        rest = refs[run.ins + run.skip :]
        rest[run.outs][...] = before[...]
        kernel(*ins, *rest[: run.outs], *rest[run.outs + 1 :])

    return run


class Order:
    def __init__(self):
        self.token = jnp.zeros((8, 128), F32)

    def call(self, name, kernel, outs, ins, scratch, limit_mib, us, aliases=None, after=()):
        run = with_token(kernel)
        run.ins, run.outs, run.skip = len(ins), len(outs), len(after)
        ins = ins + [(a, False) for a in after]
        operands = [pin(self.token)] + [place(a, where) for a, where in ins]
        *results, self.token = pl.pallas_call(
            run,
            out_shape=[o if s is VM else jax.ShapeDtypeStruct(o, F32) for o, s in outs] + [TOKEN],
            in_specs=[VM] + [{True: VM, None: HB, False: ANY}[where] for a, where in ins],
            out_specs=[s for o, s in outs] + [VM],
            scratch_shapes=scratch,
            input_output_aliases={k + 1: v for k, v in (aliases or {}).items()},
            compiler_params=pltpu.CompilerParams(vmem_limit_bytes=limit_mib << 20),
            cost_estimate=pl.CostEstimate(flops=int(us * FLOPS), bytes_accessed=0, transcendentals=0),
            name=name,
        )(*operands)
        return results


FLOPS = 7e8


def zprev(v):
    return pltpu.roll(v, 1, axis=1)


def znext(v):
    return pltpu.roll(v, NZ - 1, axis=1)


def sdown(v):
    return pltpu.roll(v, 1, axis=0)


def sup(v):
    return pltpu.roll(v, 7, axis=0)


def rows_of(buf, plane, r):
    return jnp.concatenate([buf[lane, plane, pl.ds(r, 8, stride=Q), :] for lane in range(2)], axis=-1)


def lane_copies(src_plane, dst_plane, sems):
    return [
        pltpu.make_async_copy(src_plane.at[:, pl.ds(128 * lane, 128)], dst_plane(lane), sems.at[lane])
        for lane in range(2)
    ]


def pick(table_low, table_high, node):
    return jnp.where(node == 0, jnp.float32(table_low), jnp.float32(table_high))


def own_scale(m, node):
    return pick(radau_points[m], radau_points[2 + m], node)


def inv_scale(m, node):
    return pick(1.0 / radau_points[m], 1.0 / radau_points[2 + m], node)


def weights_for(node):
    remote = [[pick(WEIGHTS[2 + m][j], WEIGHTS[m][2 + j], node) for j in range(2)] for m in range(2)]
    local = [[pick(WEIGHTS[m][j], WEIGHTS[2 + m][2 + j], node) for j in range(2)] for m in range(2)]
    return remote, local


class Rows:
    def __init__(self, k_at, y0):
        self.k_at = k_at
        self.first = y0 == 0
        self.last = y0 + ROWS == NY
        sub = lax.broadcasted_iota(jnp.int32, (8, NZ), 0)
        lane = lax.broadcasted_iota(jnp.int32, (8, NZ), 1)
        self.top = sub == 0
        self.bottom = sub == 7
        self.left = lane == 0
        self.right = lane == NZ - 1
        kc = k_at(0)
        kb = sdown(k_at(Q - 1))
        face = 0.5 * (kb + kc)
        if self.first:
            self.prev_sum = jnp.where(self.top, kc, face)
            self.prev = jnp.where(self.top, 0.0, face)
        else:
            self.prev_sum = face
            self.prev = face
        self.kc = kc

    def step(self, r):
        kc = self.kc
        kn = self.k_at(r + 1) if r < Q - 1 else sup(self.k_at(0))
        face = 0.5 * (kc + kn)
        face_sum = face
        if r == Q - 1:
            if self.last:
                face_sum = jnp.where(self.bottom, kc, face)
            face = jnp.where(self.bottom, 0.0, face)
        zface = 0.5 * (kc + znext(kc))
        zsum = jnp.where(self.right, kc, zface) + jnp.where(self.left, kc, zprev(zface))
        zface = jnp.where(self.right, 0.0, zface)
        total = self.prev_sum + face_sum + zsum
        below = self.prev
        self.prev = face
        self.prev_sum = face_sum
        self.kc = kn
        return kc, below, face, zface, total


def flux_rows(k_at, k_low, k_up, us, u_low, u_up, y0, emit):
    rows = Rows(k_at, y0)
    state = [(u(0), sdown(u(Q - 1))) for u in us]
    for r in range(Q):
        kc, below, face, zface, total = rows.step(r)
        fxl = 0.5 * (kc + k_low(r))
        fxu = 0.5 * (kc + k_up(r))
        total = total + (fxl + fxu)
        fluxes = []
        for j in range(2):
            uc, ub = state[j]
            un = us[j](r + 1) if r < Q - 1 else sup(us[j](0))
            n = fxl * u_low[j](r) + fxu * u_up[j](r)
            n = n + below * ub + face * un
            n = n + zface * znext(uc) + zprev(zface * uc)
            fluxes.append(n - total * uc)
            state[j] = (un, uc)
        emit(r, fluxes)


def inner_kernel(y0, offset0, offset1, nodes, cond, u0, kp, rem0, rem1, loc0, loc1, buf, sems):
    node = lax.axis_index("node")
    remote, local = weights_for(node)
    sources = [nodes.at[0, 0], nodes.at[0, 1], cond]

    def copies(p):
        out = []
        for a in range(3):
            out += lane_copies(
                sources[a].at[p, pl.ds(y0, ROWS), :], lambda lane, a=a: buf.at[lane, 3 * p + a], sems.at[p, a]
            )
        return out

    for p in range(PLANES):
        for c in copies(p):
            c.start()

    def convert(p, carry):
        for c in copies(p):
            c.wait()
        for r in range(Q):
            u0[p, r] = rows_of(buf, 3 * p, r)
            u0[PLANES + p, r] = rows_of(buf, 3 * p + 1, r)
            kp[p, r] = rows_of(buf, 3 * p + 2, r)
        return carry

    lax.fori_loop(0, 2, convert, 0)

    def plane(i, carry):
        p = i + 1
        convert(p + 1, carry)

        def emit(r, f):
            rem0[i + offset0, r] = remote[0][0] * f[0] + remote[0][1] * f[1]
            rem1[i + offset1, r] = remote[1][0] * f[0] + remote[1][1] * f[1]
            loc0[i, r] = local[0][0] * f[0] + local[0][1] * f[1]
            loc1[i, r] = local[1][0] * f[0] + local[1][1] * f[1]

        at = lambda j, d: (lambda r: u0[j * PLANES + p + d, r])
        flux_rows(
            lambda r: kp[p, r],
            lambda r: kp[p - 1, r],
            lambda r: kp[p + 1, r],
            [at(0, 0), at(1, 0)],
            [at(0, -1), at(1, -1)],
            [at(0, 1), at(1, 1)],
            y0,
            emit,
        )
        return carry

    lax.fori_loop(0, PLANES - 2, plane, 0)


def faces_kernel(depth, nodes, cond, sa, sb, sems):
    even = lax.rem(lax.axis_index("space"), 2) == 0

    def copies(high, low):
        pairs = []
        for dst, p in ((high, PLANES - 1 - depth), (low, depth)):
            pairs += [(cond.at[p], dst.at[0])] + [(nodes.at[0, j, p], dst.at[1 + j]) for j in range(2)]
        return [pltpu.make_async_copy(src, dst, sems.at[i]) for i, (src, dst) in enumerate(pairs)]

    @pl.when(even)
    def _():
        for c in copies(sa, sb):
            c.start()

    @pl.when(jnp.logical_not(even))
    def _():
        for c in copies(sb, sa):
            c.start()

    for c in copies(sa, sb):
        c.wait()


def halo_copies(near, planes, y0, buf, base, sems):
    out = []
    for i, p in enumerate(planes):
        out += lane_copies(
            near.at[p, pl.ds(y0, ROWS), :], lambda lane, i=i: buf.at[lane, base + i], sems.at[base + i]
        )
    return out


def begin_halos(na, nb, planes, y0, buf, sems):
    even = lax.rem(lax.axis_index("space"), 2) == 0
    n = len(planes)

    @pl.when(even)
    def _():
        for c in halo_copies(nb, planes, y0, buf, 0, sems) + halo_copies(na, planes, y0, buf, n, sems):
            c.start()

    @pl.when(jnp.logical_not(even))
    def _():
        for c in halo_copies(na, planes, y0, buf, 0, sems) + halo_copies(nb, planes, y0, buf, n, sems):
            c.start()


def end_halos(na, nb, planes, y0, buf, sems):
    for c in halo_copies(na, planes, y0, buf, 0, sems) + halo_copies(nb, planes, y0, buf, len(planes), sems):
        c.wait()


def edge_kernel(y0, at0, at1, u0, kp, na, nb, *refs):
    rem0, rem1, loc0, loc1, buf, hu, sems = refs[-7:]
    node = lax.axis_index("node")
    pos = lax.axis_index("space")
    remote, local = weights_for(node)
    planes = (0, 1, 2)
    begin_halos(na, nb, planes, y0, buf, sems)
    end_halos(na, nb, planes, y0, buf, sems)

    def convert(i, carry):
        for r in range(Q):
            hu[i, r] = rows_of(buf, i, r)
        return carry

    lax.fori_loop(0, 6, convert, 0)

    @pl.when(pos == 0)
    def _():
        hu[0] = kp[0]

    @pl.when(pos == 3)
    def _():
        hu[3] = kp[PLANES - 1]

    for e in range(2):
        p = 7 * e

        def emit(r, f, e=e):
            rem0[at0[e], r] = remote[0][0] * f[0] + remote[0][1] * f[1]
            rem1[at1[e], r] = remote[1][0] * f[0] + remote[1][1] * f[1]
            loc0[e, r] = local[0][0] * f[0] + local[0][1] * f[1]
            loc1[e, r] = local[1][0] * f[0] + local[1][1] * f[1]

        at = lambda j, d, p=p: (lambda r: u0[j * PLANES + p + d, r])
        kat = lambda d, p=p: (lambda r: kp[p + d, r])
        halo = lambda i, e=e: (lambda r: hu[3 * e + i, r])
        flux_rows(
            kat(0),
            kat(-1) if e else halo(0),
            halo(0) if e else kat(1),
            [at(0, 0), at(1, 0)],
            [at(0, -1), at(1, -1)] if e else [halo(1), halo(2)],
            [halo(1), halo(2)] if e else [at(0, 1), at(1, 1)],
            y0,
            emit,
        )


def coef_kernel(y0, kp, na, nb, fa, fb, fx, fy, fz, a0, a1, buf, far, kx, sems, far_sems):
    node = lax.axis_index("node")
    pos = lax.axis_index("space")
    begin_halos(na, nb, (0,), y0, buf, sems)
    begin_halos(fa, fb, (0,), y0, far, far_sems)

    def keep(p, carry):
        kx[p + 2] = kp[p]
        return carry

    lax.fori_loop(0, PLANES, keep, 0)
    end_halos(na, nb, (0,), y0, buf, sems)
    end_halos(fa, fb, (0,), y0, far, far_sems)

    @pl.when(pos > 0)
    def _():
        for r in range(Q):
            kx[0, r] = rows_of(far, 0, r)
            kx[1, r] = rows_of(buf, 0, r)

    @pl.when(pos == 0)
    def _():
        kx[0] = kp[0]
        kx[1] = kp[0]

    @pl.when(pos < 3)
    def _():
        for r in range(Q):
            kx[10, r] = rows_of(buf, 1, r)
            kx[11, r] = rows_of(far, 1, r)

    @pl.when(pos == 3)
    def _():
        kx[10] = kp[7]
        kx[11] = kp[7]

    inv0, inv1 = inv_scale(0, node), inv_scale(1, node)

    def coef(i, carry):
        rim = jnp.logical_or(jnp.logical_and(i == 1, pos == 0), jnp.logical_and(i == 9, pos == 3))
        open_face = jnp.where(rim, jnp.float32(0.0), jnp.float32(0.5))
        rows = Rows(lambda r: kx[i + 1, r], y0)
        for r in range(Q):
            kc, below, face, zface, total = rows.step(r)
            low = kc + kx[i, r]
            total = total + 0.5 * (low + (kc + kx[i + 2, r]))
            fx[i, r] = open_face * low
            fy[i, r] = face
            fz[i, r] = zface
            a0[i, r] = 1.0 / (inv0 + total)
            a1[i, r] = 1.0 / (inv1 + total)
        return carry

    lax.fori_loop(0, PLANES + 2, coef, 0)
    for r in range(Q):
        fx[10, r] = 0.5 * (kx[10, r] + kx[11, r])


def start_copies(src, planes, y0, buf, sems):
    out = []
    for i, p in enumerate(planes):
        out += lane_copies(src.at[p, pl.ds(y0, ROWS), :], lambda lane, i=i: buf.at[lane, i], sems.at[i])
    return out


def begin_start(prev, init, planes, y0, buf, sems):
    first = lax.axis_index("tm") == 0

    @pl.when(first)
    def _():
        for c in start_copies(init, planes, y0, buf, sems):
            c.start()

    @pl.when(jnp.logical_not(first))
    def _():
        for c in start_copies(prev, planes, y0, buf, sems):
            c.start()


def rim_kernel(where, at, *refs):
    n = len(where)
    zs, locs = refs[:n], refs[n : 2 * n]
    prev, init, rim, sa, sb, buf, sems = refs[2 * n :]
    even = lax.rem(lax.axis_index("space"), 2) == 0
    for i, y0 in enumerate(where):
        begin_start(prev, init, (0, 7), y0, buf.at[i], sems.at[i])
    for i, y0 in enumerate(where):
        for c in start_copies(prev, (0, 7), y0, buf.at[i], sems.at[i]):
            c.wait()
        for e in range(2):
            for r in range(Q):
                rim[2 * i + e, r] = rows_of(buf.at[i], e, r) + (locs[i][e, r] + zs[i][at[i][e], r])
    top = jnp.where(even, 1, 0)
    for i in range(n):
        for r in range(Q):
            sa[i, r] = rim[2 * i + top, r]
            sb[i, r] = rim[2 * i + 1 - top, r]


def sweep(src, rhs, a, fx, fy, fz, shift, count, store):
    G = 2

    def pair(t, carry):
        b = t * G
        uc = [src[b + g + 1, 0] for g in range(G)]
        last = [src[b + g + 1, Q - 1] for g in range(G)]
        flow = [sdown(fy[b + g + shift, Q - 1] * last[g]) for g in range(G)]
        for r in range(Q):
            low = src[b, r]
            high = src[b + G + 1, r]
            faces = [fx[b + g + shift, r] for g in range(G + 1)]
            column = [low] + uc + [high]
            nxt = []
            for g in range(G):
                un = src[b + g + 1, r + 1] if r < Q - 1 else sup(src[b + g + 1, 0])
                d = b + g + shift
                face = fy[d, r]
                zface = fz[d, r]
                n = faces[g] * column[g] + faces[g + 1] * column[g + 2]
                n = n + (flow[g] + face * un)
                n = n + (zface * znext(uc[g]) + zprev(zface * uc[g]))
                flow[g] = face * uc[g]
                store(b + g, r, rhs[d, r] + a[d, r] * n)
                nxt.append(un)
            uc = nxt
        return carry

    lax.fori_loop(0, count // G, pair, 0)


def two_sweeps(ub, mid, rhs, a, fx, fy, fz, store):
    def keep(d, r, value):
        mid[d, r] = value

    sweep(ub, rhs, a, fx, fy, fz, 0, PLANES + 2, keep)
    sweep(mid, rhs, a, fx, fy, fz, 1, PLANES, store)


def send_faces(u, sa, sb):
    even = lax.rem(lax.axis_index("space"), 2) == 0
    top = jnp.where(even, PLANES - 2, 0)

    def one(i, carry):
        sa[i] = u[top + i]
        sb[i] = u[PLANES - 2 - top + i]
        return carry

    lax.fori_loop(0, 2, one, 0)


def place_halo(ub, ha, hb):
    even = lax.rem(lax.axis_index("space"), 2) == 0

    def fill(low, high):
        for i in range(2):
            ub[i] = low[i]
            ub[10 + i] = high[i]

    @pl.when(even)
    def _():
        fill(hb, ha)

    @pl.when(jnp.logical_not(even))
    def _():
        fill(ha, hb)


def first_kernel(m, y0, slot, offset, z, loc, rim, ra, rb, a, fx, fy, fz, u0, prev, init, na, nb, fa, fb, rhs, u, sa, sb, ub, mid, buf, hbuf, fbuf, sems, hsems, fsems):
    node = lax.axis_index("node")
    even = lax.rem(lax.axis_index("space"), 2) == 0
    planes = tuple(range(1, PLANES - 1))
    begin_start(prev, init, planes, y0, buf, sems)
    begin_halos(na, nb, (1 + m,), y0, hbuf, hsems)
    begin_halos(fa, fb, (1 + m,), y0, fbuf, fsems)
    inv = inv_scale(m, node)

    def scaled(dst, src, at):
        for r in range(Q):
            dst[at, r] = src[r] * (a[at, r] * inv)

    @pl.when(even)
    def _():
        scaled(rhs, rb.at[slot], 0)
        scaled(rhs, ra.at[slot], 9)

    @pl.when(jnp.logical_not(even))
    def _():
        scaled(rhs, ra.at[slot], 0)
        scaled(rhs, rb.at[slot], 9)

    scaled(rhs, rim.at[2 * slot], 1)
    scaled(rhs, rim.at[2 * slot + 1], 8)

    def keep(p, carry):
        ub[p + 2] = u0[m * PLANES + p]
        return carry

    lax.fori_loop(0, PLANES, keep, 0)
    end_halos(na, nb, (1 + m,), y0, hbuf, hsems)
    end_halos(fa, fb, (1 + m,), y0, fbuf, fsems)

    def convert(i, carry):
        for r in range(Q):
            ub[1 + 9 * i, r] = rows_of(hbuf, i, r)
            ub[11 * i, r] = rows_of(fbuf, i, r)
        return carry

    lax.fori_loop(0, 2, convert, 0)
    for c in start_copies(prev, planes, y0, buf, sems):
        c.wait()

    def right(i, carry):
        for r in range(Q):
            rhs[i + 2, r] = (rows_of(buf, i, r) + (loc[i, r] + z[i + offset, r])) * (a[i + 2, r] * inv)
        return carry

    lax.fori_loop(0, PLANES - 2, right, 0)

    def store(d, r, value):
        u[d, r] = value

    two_sweeps(ub, mid, rhs, a, fx, fy, fz, store)
    send_faces(u, sa, sb)


def next_kernel(u, ha, hb, rhs, a, fx, fy, fz, unew, sa, sb, ub, mid):
    place_halo(ub, ha, hb)

    def keep(p, carry):
        ub[p + 2] = u[p]
        return carry

    lax.fori_loop(0, PLANES, keep, 0)

    def store(d, r, value):
        unew[d, r] = value

    two_sweeps(ub, mid, rhs, a, fx, fy, fz, store)
    send_faces(unew, sa, sb)


def last_kernel(m, part, aliased, u, ha, hb, rhs, a, fx, fy, fz, *rest):
    out, ub, mid, obuf, sems = rest[1:] if aliased else rest
    y0, first, kept = PARTS[part]
    place_halo(ub, ha, hb)

    def keep(p, carry):
        ub[p + 2] = u[p]
        return carry

    lax.fori_loop(0, PLANES, keep, 0)

    def store(d, r, value):
        for lane in range(2):
            obuf[lane, d, pl.ds(r, 8, stride=Q), :] = value[:, 128 * lane : 128 * lane + 128]

    two_sweeps(ub, mid, rhs, a, fx, fy, fz, store)
    cs = [
        pltpu.make_async_copy(
            obuf.at[lane, p, pl.ds(first, kept), :],
            out.at[0, m, p, pl.ds(y0 + first, kept), pl.ds(128 * lane, 128)],
            sems.at[lane, p],
        )
        for lane in range(2)
        for p in range(PLANES)
    ]
    for c in cs:
        c.start()
    for c in cs:
        c.wait()


DMA = pltpu.SemaphoreType.DMA
SWAP_A = [(0, 1), (1, 0), (2, 3), (3, 2)]
SWAP_B = [(1, 2), (2, 1)]


def to_a(x):
    return lax.ppermute(x, "space", SWAP_A)


def to_b(x):
    return lax.ppermute(x, "space", SWAP_B)


def swap_nodes(x):
    return lax.ppermute(x, "node", [(0, 1), (1, 0)])


def body(nodes, prev_final, u_init, cond):
    order = Order()

    def faces(depth):
        sa, sb = order.call(
            "faces%d" % depth,
            functools.partial(faces_kernel, depth),
            [(pltpu.VMEM((3, NY, NZ), F32), VM)] * 2,
            [(nodes, None), (cond, None)],
            [DMA((6,))],
            4,
            0.7,
        )
        return to_a(sa), to_b(sb)

    na, nb = faces(0)
    half = lax.axis_size("tm") // 2
    blocks = 2 * half
    pairs = [
        (n * blocks + t, (1 - n if t == half - 1 else n) * blocks + t + 1)
        for n in range(2)
        for t in range(blocks - 1)
    ]
    prev = lax.ppermute(prev_final[0], ("node", "tm"), pairs)

    inner, edges, coef = [], [], {}
    for part, (y0, first, kept) in enumerate(PARTS):
        inner.append(
            order.call(
                "inner%d" % part,
                functools.partial(inner_kernel, y0, part, 1 - part),
                [(vshape(n), VM) for n in (2 * PLANES, PLANES, 8 if part else 6, 6 if part else 10, 6, 6)],
                [(nodes, None), (cond, None)],
                [pltpu.VMEM((2, 3 * PLANES, ROWS, 128), F32), DMA((PLANES, 3, 2))],
                12,
                5.0,
            )
        )
    def edge_step(part):
        y0 = PARTS[part][0]
        u0, kp = inner[part][:2]
        args = [(u0, True), (kp, True), (na, False), (nb, False)]
        if part:
            args += [(inner[1][2], True), (edges[0][1], True)]
        else:
            args += [(inner[0][3], True)]
        edges.append(
            order.call(
                "edge%d" % part,
                functools.partial(edge_kernel, y0, (0, 7) if part else (0, 1), (8, 9) if part else (0, 7)),
                [(vshape(8 if part else 2), VM), (vshape(10), VM), (vshape(2), VM), (vshape(2), VM)],
                args,
                [pltpu.VMEM((2, 6, ROWS, 128), F32), pltpu.VMEM((6, Q, 8, NZ), F32), DMA((6, 2))],
                8,
                2.5,
                {4: 0, 5: 1} if part else {4: 1},
                [prev, z_start] if part else [],
            )
        )

    def coef_step(part):
        coef[part] = order.call(
            "coef%d" % part,
            functools.partial(coef_kernel, PARTS[part][0]),
            [(vshape(11), VM)] + [(vshape(10), VM)] * 4,
            [(inner[part][1], True)] + [(x, False) for x in (na, nb, fa, fb)],
            [pltpu.VMEM((2, 2, ROWS, 128), F32)] * 2 + [pltpu.VMEM((12, Q, 8, NZ), F32), DMA((2, 2)), DMA((2, 2))],
            8,
            3.5,
        )

    fa, fb = faces(1)
    z_start = swap_nodes(inner[0][2])
    edge_step(0)
    edge_step(1)

    units = [(m, part) for m in range(2) for part in range(2)]
    z_inner = [z_start] + [swap_nodes(x) for x in (edges[1][0], edges[1][1], inner[1][3])]
    z_edge = [(swap_nodes(edges[0][0]), (0, 1)), (z_inner[1], (0, 7)), (z_inner[2], (0, 7)), (z_inner[2], (8, 9))]
    state = {}
    out = [None]

    def coefs(unit):
        m, part = units[unit]
        return [(x, True) for x in [coef[part][3 + m]] + coef[part][:3]]

    def rim_step(which):
        n = len(which)
        parts = [units[unit][1] for unit in which]
        rim, ra, rb = order.call(
            "rim%d" % which[0],
            functools.partial(rim_kernel, tuple(PARTS[part][0] for part in parts), tuple(z_edge[unit][1] for unit in which)),
            [(vshape(2 * n), VM), (vshape(n), VM), (vshape(n), VM)],
            [(z_edge[unit][0], True) for unit in which]
            + [(edges[units[unit][1]][2 + units[unit][0]], True) for unit in which]
            + [(prev, False), (u_init, False)],
            [pltpu.VMEM((n, 2, 2, ROWS, 128), F32), DMA((n, 2, 2))],
            4,
            0.5,
        )
        ra, rb = to_a(ra), to_b(rb)
        for slot, unit in enumerate(which):
            state[unit] = (slot, rim, ra, rb)

    def first_step(unit):
        m, part = units[unit]
        slot, rim, ra, rb = state[unit]
        rhs, u, sa, sb = order.call(
            "first%d" % unit,
            functools.partial(first_kernel, m, PARTS[part][0], slot, 1 if unit in (1, 2) else 0),
            [(vshape(10), VM), (vshape(8), VM), (vshape(2), VM), (vshape(2), VM)],
            [(x, True) for x in (z_inner[unit], inner[part][4 + m], rim, ra, rb)]
            + coefs(unit)
            + [(inner[part][0], True)]
            + [(x, False) for x in (prev, u_init, na, nb, fa, fb)],
            [
                pltpu.VMEM((12, Q, 8, NZ), F32),
                pltpu.VMEM((10, Q, 8, NZ), F32),
                pltpu.VMEM((2, 6, ROWS, 128), F32),
                pltpu.VMEM((2, 2, ROWS, 128), F32),
                pltpu.VMEM((2, 2, ROWS, 128), F32),
                DMA((6, 2)),
                DMA((2, 2)),
                DMA((2, 2)),
            ],
            12,
            3.0,
        )
        state[unit] = (rhs, u, to_a(sa), to_b(sb))

    def next_step(unit, index):
        rhs, u, ha, hb = state[unit]
        u, sa, sb = order.call(
            "next%d_%d" % (unit, index),
            next_kernel,
            [(vshape(8), VM), (vshape(2), VM), (vshape(2), VM)],
            [(x, True) for x in (u, ha, hb, rhs)] + coefs(unit),
            [pltpu.VMEM((12, Q, 8, NZ), F32), pltpu.VMEM((10, Q, 8, NZ), F32)],
            8,
            2.5,
        )
        state[unit] = (rhs, u, to_a(sa), to_b(sb))

    def last_step(unit):
        m, part = units[unit]
        rhs, u, ha, hb = state[unit]
        args = [(x, True) for x in (u, ha, hb, rhs)] + coefs(unit)
        aliased = out[0] is not None
        if aliased:
            args.append((out[0], False))
        (out[0],) = order.call(
            "last%d" % unit,
            functools.partial(last_kernel, m, part, aliased),
            [((1, 2, PLANES, NY, NZ), ANY)],
            args,
            [
                pltpu.VMEM((12, Q, 8, NZ), F32),
                pltpu.VMEM((10, Q, 8, NZ), F32),
                pltpu.VMEM((2, 8, ROWS, 128), F32),
                DMA((2, 8)),
            ],
            8,
            3.5,
            {8: 0} if aliased else None,
        )

    C, R, S, N, M, L = range(6)
    plan = (
        (R, 0), (C, 0), (C, 1), (S, 0), (N, 0), (R, 1), (M, 0), (S, 1), (L, 0), (N, 1), (R, 2),
        (M, 1), (S, 2), (S, 3), (L, 1), (N, 2), (N, 3), (M, 2), (M, 3), (L, 2), (L, 3),
    )
    for kind, unit in plan:
        if kind == C:
            coef_step(unit)
        elif kind == R:
            rim_step((2, 3) if unit == 2 else (unit,))
        elif kind == S:
            first_step(unit)
        elif kind == L:
            last_step(unit)
        else:
            next_step(unit, kind)
    return out[0]


def solution(mesh):
    in_specs = (
        P("tm", "node", "space", None, None),
        P("tm", "space", None, None),
        P("space", None, None),
        P("space", None, None),
    )
    out_specs = P("tm", "node", "space", None, None)
    return jax.shard_map(body, mesh=mesh, in_specs=in_specs, out_specs=out_specs, check_vma=False)
```
